32 devices in a mesh: groups: 2 (over x), gx: 16 (over z, y, core).
Axes of the slice: x: 2, y: 2, z: 4, core: 2. Of those that a mesh axis runs over, the one named last changes fastest.
Arguments:
- oxygen: float32 [256, 32, 1024], P(('groups', 'gx')), parts along dimension 0, may hold values from 0.4 to 1
- potential: float32 [256, 32, 1024], P(('groups', 'gx')), parts along dimension 0, may hold values from -0.5 to 0.5
- moisture: float32 [256, 32, 1024], P(('groups', 'gx')), parts along dimension 0, may hold values from 0 to 0.2
- rate_constant: float32 [256, 32, 1024], P(('groups', 'gx')), parts along dimension 0, may hold values from 0.5 to 2
- cell_labels: int32 [256, 32, 1024], P(('groups', 'gx')), parts along dimension 0, may hold values from 0 to 2, as said below
- current_density: float32 [2], P('groups'), parts along dimension 0, may hold values from 0.6 to 1.2
Outputs:
- oxygen_out: float32 [256, 32, 1024], P(('groups', 'gx')), parts along dimension 0
- potential_out: float32 [256, 32, 1024], P(('groups', 'gx')), parts along dimension 0
- moisture_out: float32 [256, 32, 1024], P(('groups', 'gx')), parts along dimension 0
The draws below stay inside these ranges and needn't reach their ends.
There are 2 independent parts, one for each index of `groups`. The reference program is written for one: setup_inputs(seed, part) draws one part's arguments, and reference() takes and returns one part's arrays. A program takes and returns all parts, laid end to end along the dimension named above; each array names one. Nothing has to cross between parts.
Inputs may be any that keep to these rules, and one draw needn't show every extreme that they name: `cell_labels`: each cell is 0 (solid carbon), 1 (pore) or 2 (ionomer-covered wall); the shares of pore and wall cells differ between bricks of 8 rows along the first dimension.
All inputs are finite; a program needn't handle non-finite values.
Results may differ from the reference program's by a relative error of at most 0.0001.
Values sent between devices are 32-bit elements; how exact they have to be, the bound alone decides.
A program may use at most 64 MiB of HBM per device.

```python
import math
import jax
import jax.numpy as jnp
from jax import lax

CX = 8
NY = 1024
NZ = 32
SUBSTEPS = 2
NX = 128


def draw_cell_labels(key, part):
    key = jax.random.fold_in(key, 11)
    roll = jax.random.randint(key, (NX, NZ, NY), 0, 1000)
    bricks = NX // CX
    spread = max(bricks - 1, 1)
    brick_index = lax.broadcasted_iota(jnp.int32, (NX, 1, 1), 0) // CX
    pore_cut = 150 + 300 * brick_index // spread
    wall_cut = pore_cut + 100 + 200 * brick_index // spread
    return jnp.where(roll < pore_cut, 1, jnp.where(roll < wall_cut, 2, 0)).astype(jnp.int32)


def draw_potential(key, part):
    key = jax.random.fold_in(key, 23)
    rough_key = jax.random.fold_in(key, 1)
    offset_key = jax.random.fold_in(key, 2)
    rough = jax.random.uniform(rough_key, (NX, NZ, NY), jnp.float32, -1.0, 1.0)
    offset = jax.random.uniform(offset_key, (), jnp.float32, -0.2, 0.2)
    return jnp.clip(offset + 0.45 * rough, -0.5, 0.5).astype(jnp.float32)


def level_of(stream_key, extent, pieces, smallest, top_value):
    gain = 1.0
    for axis_at, shards_of in pieces:
        steps = jax.random.uniform(jax.random.fold_in(jax.random.fold_in(stream_key, 6), axis_at), (shards_of,), jnp.float32, smallest / len(pieces), top_value / len(pieces))
        gain = gain * jnp.repeat(jnp.exp(steps), extent[axis_at] // shards_of).reshape((-1,) + (1,) * (len(extent) - 1 - axis_at))
    return gain


def setup_inputs(seed: int = 0, part: int = 0) -> dict:
    keys = jax.random.split(jax.random.key(seed), 7)
    part_keys = jax.random.split(jax.random.fold_in(keys[6], part), 7)
    return {
        "oxygen": jnp.clip(0.4 + 0.6 * jax.random.uniform(part_keys[0], (NX, NZ, NY), jnp.float32) ** level_of(part_keys[0], (NX, NZ, NY), ((0, 16),), -0.2, 0.2), 0.4, 1.0),
        "potential": draw_potential(jax.random.fold_in(jax.random.fold_in(keys[6], part), 71), part),
        "moisture": jnp.clip(0.2 * jax.random.uniform(part_keys[2], (NX, NZ, NY), jnp.float32) ** level_of(part_keys[2], (NX, NZ, NY), ((0, 16),), -0.2, 0.2), 0.0, 0.2),
        "rate_constant": jnp.clip(jnp.exp(math.log(2.0) - 1.3862944 * jax.random.uniform(part_keys[3], (NX, NZ, NY), jnp.float32) ** level_of(part_keys[3], (NX, NZ, NY), ((0, 16),), -0.2, 0.2)), 0.5, 2.0),
        "cell_labels": draw_cell_labels(jax.random.fold_in(jax.random.fold_in(keys[6], part), 71), part),
        "current_density": jnp.clip(jax.random.uniform(part_keys[5], (1,), jnp.float32, 0.6, 1.2), 0.6, 1.2),
    }


def neighbours(field):
    middle = field[1:-1]
    summed = field[2:] + field[:-2]
    padded_z = jnp.pad(middle, ((0, 0), (1, 1), (0, 0)))
    summed = summed + padded_z[:, 2:] + padded_z[:, :-2]
    padded_y = jnp.pad(middle, ((0, 0), (0, 0), (1, 1)))
    return summed + padded_y[:, :, 2:] + padded_y[:, :, :-2]


def diffuse(field, weights):
    return weights[1:-1] * (neighbours(weights * field) - field[1:-1] * neighbours(weights))


def pad_rows(field):
    return jnp.pad(field, ((1, 1), (0, 0), (0, 0)))


def reference(oxygen, potential, moisture, rate_constant, cell_labels, current_density):
    open_m = (cell_labels >= 1).astype(jnp.float32)
    wall_m = (cell_labels == 2).astype(jnp.float32)
    depth_index = lax.broadcasted_iota(jnp.int32, (1, NZ, 1), 1)
    top_m = (depth_index == 0).astype(jnp.float32)
    bottom_m = (depth_index == NZ - 1).astype(jnp.float32)
    electrode_shift = jnp.zeros((), jnp.float32)
    for substep in range(SUBSTEPS):
        overpotential = electrode_shift - potential
        forward = jnp.exp(1.5 * overpotential)
        backward = jnp.exp(-1.5 * overpotential)
        resid = jnp.sum(wall_m * (rate_constant * (oxygen * forward - backward) - current_density[0]))
        slope = jnp.sum(wall_m * rate_constant * (1.5 * oxygen * forward + 1.5 * backward))
        electrode_shift = electrode_shift - resid / slope
        overpotential = electrode_shift - potential
        reaction = wall_m * rate_constant * (oxygen * jnp.exp(1.5 * overpotential) - jnp.exp(-1.5 * overpotential))
        soaking = 1.0 / (1.0 + moisture * moisture)
        new_oxygen = oxygen + 0.16 * diffuse(pad_rows(oxygen), pad_rows(open_m * soaking)) + 0.16 * top_m * open_m * (1.0 - oxygen) - 0.04 * reaction
        new_potential = potential + 0.15 * diffuse(pad_rows(potential), pad_rows(wall_m)) - 0.15 * bottom_m * wall_m * potential - 0.3 * reaction
        new_moisture = moisture + 0.12 * diffuse(pad_rows(moisture), pad_rows(open_m)) - 0.12 * top_m * open_m * moisture + 0.06 * reaction
        oxygen, potential, moisture = new_oxygen, new_potential, new_moisture
    return oxygen, potential, moisture
```

```python
import functools
import math

import jax
import jax.numpy as jnp
from jax import lax
from jax.experimental import pallas as pl
from jax.experimental.pallas import tpu as pltpu
from jax.sharding import PartitionSpec as P

MESH = pl.DeviceIdType.MESH
LOG = 1.5 * math.log2(math.e)
PAD = 8


def kernel(
    n, rows, layers, width,
    c_in, p_in, m_in, k_in, l_in, density,
    c_out, p_out, m_out,
    c0, p0, m0, q0, lab, c1, p1, m1, q1, rate, fwd, bwd, part, gathered,
    load_sem, store_sem, send_sem, recv_sem, part_send, part_recv,
):
    group = lax.axis_index("groups")
    me = lax.axis_index("gx")
    left, right = lax.rem(me + n - 1, n), lax.rem(me + 1, n)
    tiles = layers // 8
    last = rows + 1
    first = (c0, p0, m0)
    second = (c1, p1, m1)
    ins = (c_in, p_in, m_in, l_in)
    outs = (c_out, p_out, m_out)

    loads = [
        pltpu.make_async_copy(src, dst.at[pl.ds(1, rows), pl.ds(PAD, layers), :], load_sem.at[i])
        for i, (src, dst) in enumerate(((c_in, c0), (p_in, p0), (l_in, lab), (m_in, m0)))
    ]
    loads.append(pltpu.make_async_copy(k_in, rate, load_sem.at[4]))
    for copy in loads:
        copy.start()

    barrier = pltpu.get_barrier_semaphore()

    @pl.loop(1, n)
    def _(d):
        pl.semaphore_signal(
            barrier, inc=1, device_id=(group, lax.rem(me + d, n)), device_id_type=MESH
        )

    def halo(step, way, f, j):
        z = pl.ds(PAD + 8 * j, 8)
        if step == 0:
            src = ins[f].at[0 if way == 0 else rows - 1, pl.ds(8 * j, 8), :]
            dst = (c0, p0, m0, lab)[f]
        else:
            src = second[f].at[1 if way == 0 else rows, z, :]
            dst = second[f]
        return pltpu.make_async_remote_copy(
            src_ref=src,
            dst_ref=dst.at[last if way == 0 else 0, z, :],
            send_sem=send_sem.at[step, way, f, j],
            recv_sem=recv_sem.at[step, way, f, j],
            device_id=(group, left if way == 0 else right),
            device_id_type=MESH,
        )

    has_left = me > 0
    has_right = me < n - 1

    for ref in (c0, p0, m0, q0, lab, c1, p1, m1, q1):
        zero = jnp.zeros((rows + 2, 8, width), ref.dtype)
        ref[:, 0:PAD, :] = zero
        ref[:, PAD + layers :, :] = zero

    @pl.when(jnp.logical_not(has_left))
    def _():
        for ref in (c0, p0, m0, lab, c1, p1, m1):
            ref[0, PAD : PAD + layers, :] = jnp.zeros((layers, width), ref.dtype)

    @pl.when(jnp.logical_not(has_right))
    def _():
        for ref in (c0, p0, m0, lab, c1, p1, m1):
            ref[last, PAD : PAD + layers, :] = jnp.zeros((layers, width), ref.dtype)

    pl.semaphore_wait(barrier, n - 1)

    for j in range(tiles):
        for f in range(4):
            @pl.when(has_left)
            def _():
                halo(0, 0, f, j).start()

            @pl.when(has_right)
            def _():
                halo(0, 1, f, j).start()

    for copy in loads:
        copy.wait()

    def fold(v):
        total = v[:, 0:128]
        for at in range(128, width, 128):
            total = total + v[:, at : at + 128]
        return total

    def soak(labels, m):
        return jnp.where(labels >= 1, 1.0 / (1.0 + m * m), 0.0)

    def exchange(labels, c, p, x, z, shift):
        power = (shift - p) * LOG
        is_wall = labels == 2
        k = jnp.where(is_wall, rate[x - 1, pl.ds(z - PAD, 8), :], 0.0)
        forward = k * c * jnp.exp2(power)
        backward = k * jnp.exp2(-power)
        fwd[x - 1, pl.ds(z - PAD, 8), :] = forward
        bwd[x - 1, pl.ds(z - PAD, 8), :] = backward
        return fold(forward), fold(backward), fold(jnp.where(is_wall, 1.0, 0.0))

    def sum_start(step, sums):
        row = lax.broadcasted_iota(jnp.int32, (8, 128), 0)
        a, b, w = (jnp.sum(s, axis=0, keepdims=True) for s in sums)
        part[step] = jnp.where(row == 0, a, jnp.where(row == 1, b, jnp.where(row == 2, w, 0.0)))

        @pl.loop(1, n)
        def _(d):
            pltpu.make_async_remote_copy(
                src_ref=part.at[step],
                dst_ref=gathered.at[step, d - 1],
                send_sem=part_send.at[step],
                recv_sem=part_recv.at[step],
                device_id=(group, lax.rem(me + d, n)),
                device_id_type=MESH,
            ).start()

    def sum_finish(step):
        all_parts = gathered.at[step]
        pltpu.make_async_copy(all_parts, all_parts, part_recv.at[step]).wait()
        total = part[step] + jnp.sum(gathered[step], axis=0)
        a, b, w = (jnp.sum(total[i : i + 1, :], axis=1, keepdims=True) for i in range(3))
        delta = (density[0] * w + b - a) / (1.5 * (a + b))
        return delta, jnp.exp2(delta * LOG), jnp.exp2(-delta * LOG)

    def spread(src, q, x, i):
        z = PAD + 8 * i
        c_ref, p_ref, m_ref = src
        here = pl.ds(z, 8)
        c, p, m, labels, weight = (r[x, here, :] for r in (c_ref, p_ref, m_ref, lab, q))
        lane = lax.broadcasted_iota(jnp.int32, (8, width), 1)
        near = []
        for at in ((x - 1, here), (x + 1, here), (x, pl.ds(z - 1, 8)), (x, pl.ds(z + 1, 8))):
            near.append(tuple(r[at[0], at[1], :] for r in (c_ref, p_ref, m_ref, lab, q)))
        for shift, edge in ((1, 0), (width - 1, width - 1)):
            cb, pb, mb, lb, qb = (pltpu.roll(v, shift, 1) for v in (c, p, m, labels, weight))
            near.append((cb, pb, mb, jnp.where(lane == edge, 0, lb), jnp.where(lane == edge, 0.0, qb)))
        dc = dp = dm = None
        for cb, pb, mb, lb, qb in near:
            tc = qb * (cb - c)
            tp = jnp.where(lb == 2, pb - p, 0.0)
            tm = jnp.where(lb >= 1, mb - m, 0.0)
            dc, dp, dm = (tc, tp, tm) if dc is None else (dc + tc, dp + tp, dm + tm)
        is_open, is_wall = labels >= 1, labels == 2
        dc = weight * dc
        if i == 0:
            top = lax.broadcasted_iota(jnp.int32, (8, width), 0) == 0
            dm = jnp.where(top, dm - m, dm)
            dc = dc + jnp.where(jnp.logical_and(top, is_open), 1.0 - c, 0.0)
        if i == tiles - 1:
            bottom = lax.broadcasted_iota(jnp.int32, (8, width), 0) == 7
            dp = jnp.where(bottom, dp - p, dp)
        c = c + 0.16 * dc
        p = p + jnp.where(is_wall, 0.15 * dp, 0.0)
        m = m + jnp.where(is_open, 0.12 * dm, 0.0)
        return c, p, m

    def react(values, x, i, up, down):
        c, p, m = values
        z = pl.ds(8 * i, 8)
        reaction = fwd[x - 1, z, :] * up - bwd[x - 1, z, :] * down
        return c - 0.04 * reaction, p - 0.3 * reaction, m + 0.06 * reaction

    def put(dst, x, i, values):
        for ref, value in zip(dst, values):
            ref[x, pl.ds(PAD + 8 * i, 8), :] = value

    def get(src, x, i):
        return tuple(ref[x, pl.ds(PAD + 8 * i, 8), :] for ref in src)

    def add(sums, more):
        return tuple(s + t for s, t in zip(sums, more))

    none = (jnp.zeros((8, 128), jnp.float32),) * 3

    def opening(x, sums):
        for i in range(tiles):
            z = PAD + 8 * i
            c, p, m = get(first, x, i)
            labels = lab[x, pl.ds(z, 8), :]
            q0[x, pl.ds(z, 8), :] = soak(labels, m)
            sums = add(sums, exchange(labels, c, p, x, z, 0.0))
        return sums

    sum_start(0, lax.fori_loop(1, rows + 1, opening, none))

    @pl.loop(2, rows)
    def _(x):
        for i in range(tiles):
            put(second, x, i, spread(first, q0, x, i))

    shift, up, down = sum_finish(0)
    shift_s, up_s, down_s = shift[0, 0], up[0, 0], down[0, 0]

    def settle(values, x, i):
        z = PAD + 8 * i
        c, p, m = react(values, x, i, up_s, down_s)
        put(second, x, i, (c, p, m))
        labels = lab[x, pl.ds(z, 8), :]
        q1[x, pl.ds(z, 8), :] = soak(labels, m)
        return exchange(labels, c, p, x, z, shift_s)

    def inner(x, sums):
        for i in range(tiles):
            sums = add(sums, settle(get(second, x, i), x, i))
        return sums

    sums = lax.fori_loop(2, rows, inner, none)

    sides = ((0, 1, 1, has_left), (last, rows, 0, has_right))
    for i in range(tiles):
        for outer, x, way, present in sides:
            @pl.when(present)
            def _():
                for f in range(4):
                    halo(0, way, f, i).wait_recv()

            z = pl.ds(PAD + 8 * i, 8)
            q0[outer, z, :] = soak(lab[outer, z, :], m0[outer, z, :])
            sums = add(sums, settle(spread(first, q0, x, i), x, i))

            @pl.when(present)
            def _():
                for f in range(3):
                    halo(1, 1 - way, f, i).start()

    sum_start(1, sums)

    @pl.loop(2, rows)
    def _(x):
        for i in range(tiles):
            put(first, x, i, spread(second, q1, x, i))

    _, up, down = sum_finish(1)
    up_f, down_f = up[0, 0], down[0, 0]

    @pl.loop(2, rows)
    def _(x):
        for i in range(tiles):
            put(first, x, i, react(get(first, x, i), x, i, up_f, down_f))

    stores = []
    for f in range(3):
        stores.append(
            pltpu.make_async_copy(
                first[f].at[pl.ds(2, rows - 2), pl.ds(PAD, layers), :],
                outs[f].at[pl.ds(1, rows - 2), :, :],
                store_sem.at[f, 0],
            )
        )
        stores[-1].start()

    for i in range(tiles):
        for outer, x, way, present in sides:
            @pl.when(present)
            def _():
                for f in range(3):
                    halo(1, way, f, i).wait_recv()

            z = pl.ds(PAD + 8 * i, 8)
            q1[outer, z, :] = soak(lab[outer, z, :], m1[outer, z, :])
            put(first, x, i, react(spread(second, q1, x, i), x, i, up_f, down_f))

    for f in range(3):
        for s, x in enumerate((1, rows)):
            stores.append(
                pltpu.make_async_copy(
                    first[f].at[x, pl.ds(PAD, layers), :], outs[f].at[x - 1], store_sem.at[f, 1 + s]
                )
            )
            stores[-1].start()

    for step in range(2):
        pltpu.make_async_copy(gathered.at[step], gathered.at[step], part_send.at[step]).wait()
        for outer, x, way, present in sides:
            @pl.when(present)
            def _():
                for i in range(tiles):
                    for f in range(4 - step):
                        halo(step, 1 - way, f, i).wait_send()
    for copy in stores:
        copy.wait()


def solution(mesh):
    n = mesh.shape["gx"]

    def on_device(oxygen, potential, moisture, rate_constant, cell_labels, current_density):
        rows, layers, width = oxygen.shape
        tiles = layers // 8
        padded = (rows + 2, layers + 2 * PAD, width)
        big = pltpu.VMEM(padded, jnp.float32)
        own = pltpu.VMEM((rows, layers, width), jnp.float32)
        hbm = pl.BlockSpec(memory_space=pl.ANY)
        return pl.pallas_call(
            functools.partial(kernel, n, rows, layers, width),
            out_shape=[jax.ShapeDtypeStruct((rows, layers, width), jnp.float32)] * 3,
            in_specs=[hbm] * 5 + [pl.BlockSpec(memory_space=pltpu.SMEM)],
            out_specs=[hbm] * 3,
            scratch_shapes=[
                big, big, big, big, pltpu.VMEM(padded, jnp.int32),
                big, big, big, big,
                own, own, own,
                pltpu.VMEM((2, 8, 128), jnp.float32),
                pltpu.VMEM((2, n - 1, 8, 128), jnp.float32),
                pltpu.SemaphoreType.DMA((5,)),
                pltpu.SemaphoreType.DMA((3, 3)),
                pltpu.SemaphoreType.DMA((2, 2, 4, tiles)),
                pltpu.SemaphoreType.DMA((2, 2, 4, tiles)),
                pltpu.SemaphoreType.DMA((2,)),
                pltpu.SemaphoreType.DMA((2,)),
            ],
            compiler_params=pltpu.CompilerParams(
                collective_id=0, has_side_effects=True, vmem_limit_bytes=48 * 1024 * 1024
            ),
        )(oxygen, potential, moisture, rate_constant, cell_labels, current_density)

    field = P(("groups", "gx"), None, None)
    return jax.shard_map(
        on_device,
        mesh=mesh,
        in_specs=(field,) * 5 + (P("groups"),),
        out_specs=(field,) * 3,
        check_vma=False,
    )
```

```python
import functools
import math

import jax
import jax.numpy as jnp
from jax import lax
from jax.experimental import pallas as pl
from jax.experimental.pallas import tpu as pltpu
from jax.sharding import PartitionSpec as P

MESH = pl.DeviceIdType.MESH
LOG = 1.5 * math.log2(math.e)
PAD = 8
AHEAD = 2


def kernel(
    n, rows, layers, width,
    c_in, p_in, m_in, k_in, l_in, density,
    c_out, p_out, m_out,
    c0, p0, m0, q0, lab, c1, p1, m1, q1, rate, fwd, bwd, part, gathered,
    load_sem, store_sem, send_sem, recv_sem, part_send, part_recv,
):
    group = lax.axis_index("groups")
    me = lax.axis_index("gx")
    left, right = lax.rem(me + n - 1, n), lax.rem(me + 1, n)
    tiles = layers // 8
    last = rows + 1
    first = (c0, p0, m0)
    second = (c1, p1, m1)
    ins = (c_in, p_in, m_in, l_in)
    outs = (c_out, p_out, m_out)

    loads = [
        pltpu.make_async_copy(src, dst.at[pl.ds(1, rows), pl.ds(PAD, layers), :], load_sem.at[i])
        for i, (src, dst) in enumerate(((c_in, c0), (p_in, p0), (l_in, lab), (m_in, m0)))
    ]
    loads.append(pltpu.make_async_copy(k_in, rate, load_sem.at[4]))
    for copy in loads:
        copy.start()

    barrier = pltpu.get_barrier_semaphore()

    @pl.loop(1, n)
    def _(d):
        pl.semaphore_signal(
            barrier, inc=1, device_id=(group, lax.rem(me + d, n)), device_id_type=MESH
        )

    def halo(step, way, f, j):
        z = pl.ds(PAD + 8 * j, 8)
        if step == 0:
            src = ins[f].at[0 if way == 0 else rows - 1, pl.ds(8 * j, 8), :]
            dst = (c0, p0, m0, lab)[f]
        else:
            src = second[f].at[1 if way == 0 else rows, z, :]
            dst = second[f]
        return pltpu.make_async_remote_copy(
            src_ref=src,
            dst_ref=dst.at[last if way == 0 else 0, z, :],
            send_sem=send_sem.at[step, way, f, j],
            recv_sem=recv_sem.at[step, way, f, j],
            device_id=(group, left if way == 0 else right),
            device_id_type=MESH,
        )

    has_left = me > 0
    has_right = me < n - 1

    for ref in (c0, p0, m0, q0, lab, c1, p1, m1, q1):
        zero = jnp.zeros((rows + 2, 8, width), ref.dtype)
        ref[:, 0:PAD, :] = zero
        ref[:, PAD + layers :, :] = zero

    @pl.when(jnp.logical_not(has_left))
    def _():
        for ref in (c0, p0, m0, lab, c1, p1, m1):
            ref[0, PAD : PAD + layers, :] = jnp.zeros((layers, width), ref.dtype)

    @pl.when(jnp.logical_not(has_right))
    def _():
        for ref in (c0, p0, m0, lab, c1, p1, m1):
            ref[last, PAD : PAD + layers, :] = jnp.zeros((layers, width), ref.dtype)

    pl.semaphore_wait(barrier, n - 1)

    def send_rows(j):
        for f in range(4):
            @pl.when(has_left)
            def _():
                halo(0, 0, f, j).start()

            @pl.when(has_right)
            def _():
                halo(0, 1, f, j).start()

    for j in range(AHEAD):
        send_rows(j)

    for copy in loads:
        copy.wait()

    def fold(v):
        total = v[:, 0:128]
        for at in range(128, width, 128):
            total = total + v[:, at : at + 128]
        return total

    def soak(labels, m):
        return jnp.where(labels >= 1, 1.0 / (1.0 + m * m), 0.0)

    def exchange(labels, c, p, x, z, shift):
        power = (shift - p) * LOG
        is_wall = labels == 2
        k = jnp.where(is_wall, rate[x - 1, pl.ds(z - PAD, 8), :], 0.0)
        forward = k * c * jnp.exp2(power)
        backward = k * jnp.exp2(-power)
        fwd[x - 1, pl.ds(z - PAD, 8), :] = forward
        bwd[x - 1, pl.ds(z - PAD, 8), :] = backward
        return fold(forward), fold(backward), fold(jnp.where(is_wall, 1.0, 0.0))

    def sum_start(step, sums):
        lane = lax.broadcasted_iota(jnp.int32, (1, 128), 1)
        a, b, w = (jnp.sum(jnp.sum(s, axis=0, keepdims=True), axis=1, keepdims=True) for s in sums)
        part[step] = jnp.where(lane == 0, a, jnp.where(lane == 1, b, jnp.where(lane == 2, w, 0.0)))

        @pl.loop(1, n)
        def _(d):
            pltpu.make_async_remote_copy(
                src_ref=part.at[step],
                dst_ref=gathered.at[step, d - 1],
                send_sem=part_send.at[step],
                recv_sem=part_recv.at[step],
                device_id=(group, lax.rem(me + d, n)),
                device_id_type=MESH,
            ).start()

    def sum_finish(step):
        all_parts = gathered.at[step]
        pltpu.make_async_copy(all_parts, all_parts, part_recv.at[step]).wait()
        total = part[step] + jnp.sum(gathered[step], axis=0)
        a, b, w = (total[:, i : i + 1] for i in range(3))
        delta = (density[0] * w + b - a) / (1.5 * (a + b))
        return delta, jnp.exp2(delta * LOG), jnp.exp2(-delta * LOG)

    def spread(src, q, x, i):
        z = PAD + 8 * i
        c_ref, p_ref, m_ref = src
        here = pl.ds(z, 8)
        c, p, m, labels, weight = (r[x, here, :] for r in (c_ref, p_ref, m_ref, lab, q))
        lane = lax.broadcasted_iota(jnp.int32, (8, width), 1)
        near = []
        for at in ((x - 1, here), (x + 1, here), (x, pl.ds(z - 1, 8)), (x, pl.ds(z + 1, 8))):
            near.append(tuple(r[at[0], at[1], :] for r in (c_ref, p_ref, m_ref, lab, q)))
        for shift, edge in ((1, 0), (width - 1, width - 1)):
            cb, pb, mb, lb, qb = (pltpu.roll(v, shift, 1) for v in (c, p, m, labels, weight))
            near.append((cb, pb, mb, jnp.where(lane == edge, 0, lb), jnp.where(lane == edge, 0.0, qb)))
        dc = dp = dm = None
        for cb, pb, mb, lb, qb in near:
            tc = qb * (cb - c)
            tp = jnp.where(lb == 2, pb - p, 0.0)
            tm = jnp.where(lb >= 1, mb - m, 0.0)
            dc, dp, dm = (tc, tp, tm) if dc is None else (dc + tc, dp + tp, dm + tm)
        is_open, is_wall = labels >= 1, labels == 2
        dc = weight * dc
        if i == 0:
            top = lax.broadcasted_iota(jnp.int32, (8, width), 0) == 0
            dm = jnp.where(top, dm - m, dm)
            dc = dc + jnp.where(jnp.logical_and(top, is_open), 1.0 - c, 0.0)
        if i == tiles - 1:
            bottom = lax.broadcasted_iota(jnp.int32, (8, width), 0) == 7
            dp = jnp.where(bottom, dp - p, dp)
        c = c + 0.16 * dc
        p = p + jnp.where(is_wall, 0.15 * dp, 0.0)
        m = m + jnp.where(is_open, 0.12 * dm, 0.0)
        return c, p, m

    def react(values, x, i, up, down):
        c, p, m = values
        z = pl.ds(8 * i, 8)
        reaction = fwd[x - 1, z, :] * up - bwd[x - 1, z, :] * down
        return c - 0.04 * reaction, p - 0.3 * reaction, m + 0.06 * reaction

    def put(dst, x, i, values):
        for ref, value in zip(dst, values):
            ref[x, pl.ds(PAD + 8 * i, 8), :] = value

    def get(src, x, i):
        return tuple(ref[x, pl.ds(PAD + 8 * i, 8), :] for ref in src)

    def add(sums, more):
        return tuple(s + t for s, t in zip(sums, more))

    none = (jnp.zeros((8, 128), jnp.float32),) * 3

    def opening(x, sums):
        for i in range(tiles):
            z = PAD + 8 * i
            c, p, m = get(first, x, i)
            labels = lab[x, pl.ds(z, 8), :]
            q0[x, pl.ds(z, 8), :] = soak(labels, m)
            sums = add(sums, exchange(labels, c, p, x, z, 0.0))
        return sums

    sum_start(0, lax.fori_loop(1, rows + 1, opening, none))
    for j in range(AHEAD, tiles):
        send_rows(j)

    @pl.loop(2, rows)
    def _(x):
        for i in range(tiles):
            put(second, x, i, spread(first, q0, x, i))

    shift, up, down = sum_finish(0)
    shift_s, up_s, down_s = shift[0, 0], up[0, 0], down[0, 0]

    def settle(values, x, i):
        z = PAD + 8 * i
        c, p, m = react(values, x, i, up_s, down_s)
        put(second, x, i, (c, p, m))
        labels = lab[x, pl.ds(z, 8), :]
        q1[x, pl.ds(z, 8), :] = soak(labels, m)
        return exchange(labels, c, p, x, z, shift_s)

    def inner(i, sums):
        return lax.fori_loop(2, rows, lambda x, s: add(s, settle(get(second, x, i), x, i)), sums)

    sums = none
    sides = ((0, 1, 1, has_left), (last, rows, 0, has_right))
    for i in range(tiles):
        if i == tiles - 1:
            sums = inner(i, sums)
        for outer, x, way, present in sides:
            @pl.when(present)
            def _():
                for f in range(4):
                    halo(0, way, f, i).wait_recv()

            z = pl.ds(PAD + 8 * i, 8)
            q0[outer, z, :] = soak(lab[outer, z, :], m0[outer, z, :])
            sums = add(sums, settle(spread(first, q0, x, i), x, i))

            @pl.when(present)
            def _():
                for f in range(3):
                    halo(1, 1 - way, f, i).start()

        if i < tiles - 1:
            sums = inner(i, sums)

    sum_start(1, sums)

    @pl.loop(2, rows)
    def _(x):
        for i in range(tiles):
            put(first, x, i, spread(second, q1, x, i))

    _, up, down = sum_finish(1)
    up_f, down_f = up[0, 0], down[0, 0]

    @pl.loop(2, rows)
    def _(x):
        for i in range(tiles):
            put(first, x, i, react(get(first, x, i), x, i, up_f, down_f))

    stores = []
    for f in range(3):
        stores.append(
            pltpu.make_async_copy(
                first[f].at[pl.ds(2, rows - 2), pl.ds(PAD, layers), :],
                outs[f].at[pl.ds(1, rows - 2), :, :],
                store_sem.at[f, 0],
            )
        )
        stores[-1].start()

    for i in range(tiles):
        for outer, x, way, present in sides:
            @pl.when(present)
            def _():
                for f in range(3):
                    halo(1, way, f, i).wait_recv()

            z = pl.ds(PAD + 8 * i, 8)
            q1[outer, z, :] = soak(lab[outer, z, :], m1[outer, z, :])
            put(first, x, i, react(spread(second, q1, x, i), x, i, up_f, down_f))

    for f in range(3):
        for s, x in enumerate((1, rows)):
            stores.append(
                pltpu.make_async_copy(
                    first[f].at[x, pl.ds(PAD, layers), :], outs[f].at[x - 1], store_sem.at[f, 1 + s]
                )
            )
            stores[-1].start()

    for step in range(2):
        pltpu.make_async_copy(gathered.at[step], gathered.at[step], part_send.at[step]).wait()
        for outer, x, way, present in sides:
            @pl.when(present)
            def _():
                for i in range(tiles):
                    for f in range(4 - step):
                        halo(step, 1 - way, f, i).wait_send()
    for copy in stores:
        copy.wait()


def hand_out(*refs):
    sources, targets, held, sem = refs[:3], refs[3:6], refs[6:9], refs[9]
    q = sources[0].shape[0] // 4
    todo = []
    for h in range(4):
        for f in range(3):
            piece = pl.ds(h * q, q)
            a = pltpu.make_async_copy(sources[f].at[piece], held[f].at[piece], sem.at[0, f, h])
            b = pltpu.make_async_copy(held[f].at[piece], targets[f].at[piece], sem.at[1, f, h])
            a.start()
            todo.append((a, b))
    for a, b in todo:
        a.wait()
        b.start()
    for a, b in todo:
        b.wait()


def solution(mesh):
    n = mesh.shape["gx"]

    def on_device(oxygen, potential, moisture, rate_constant, cell_labels, current_density):
        rows, layers, width = oxygen.shape
        tiles = layers // 8
        padded = (rows + 2, layers + 2 * PAD, width)
        big = pltpu.VMEM(padded, jnp.float32)
        own = pltpu.VMEM((rows, layers, width), jnp.float32)
        hbm = pl.BlockSpec(memory_space=pl.ANY)
        pinned = pl.BlockSpec(memory_space=pltpu.HBM)
        fields = pl.pallas_call(
            functools.partial(kernel, n, rows, layers, width),
            out_shape=[jax.ShapeDtypeStruct((rows, layers, width), jnp.float32)] * 3,
            in_specs=[pinned] * 5 + [pl.BlockSpec(memory_space=pltpu.SMEM)],
            out_specs=[hbm] * 3,
            scratch_shapes=[
                big, big, big, big, pltpu.VMEM(padded, jnp.int32),
                big, big, big, big,
                own, own, own,
                pltpu.VMEM((2, 1, 128), jnp.float32),
                pltpu.VMEM((2, n - 1, 1, 128), jnp.float32),
                pltpu.SemaphoreType.DMA((5,)),
                pltpu.SemaphoreType.DMA((3, 3)),
                pltpu.SemaphoreType.DMA((2, 2, 4, tiles)),
                pltpu.SemaphoreType.DMA((2, 2, 4, tiles)),
                pltpu.SemaphoreType.DMA((2,)),
                pltpu.SemaphoreType.DMA((2,)),
            ],
            compiler_params=pltpu.CompilerParams(
                collective_id=0, has_side_effects=True, vmem_limit_bytes=63 * 1024 * 1024 + 512 * 1024
            ),
        )(oxygen, potential, moisture, rate_constant, cell_labels, current_density)
        return pl.pallas_call(
            hand_out,
            out_shape=[jax.ShapeDtypeStruct((rows, layers, width), jnp.float32)] * 3,
            in_specs=[hbm] * 3,
            out_specs=[pinned] * 3,
            scratch_shapes=[own, own, own, pltpu.SemaphoreType.DMA((2, 3, 4))],
            compiler_params=pltpu.CompilerParams(vmem_limit_bytes=62 * 1024 * 1024),
        )(*fields)

    field = P(("groups", "gx"), None, None)
    return jax.shard_map(
        on_device,
        mesh=mesh,
        in_specs=(field,) * 5 + (P("groups"),),
        out_specs=(field,) * 3,
        check_vma=False,
    )
```

```python
import functools
import math

import jax
import jax.numpy as jnp
from jax import lax
from jax.experimental import pallas as pl
from jax.experimental.pallas import tpu as pltpu
from jax.sharding import PartitionSpec as P

MESH = pl.DeviceIdType.MESH
LOG = 1.5 * math.log2(math.e)
PAD = 8
AHEAD = 2


def kernel(
    n, rows, layers, width,
    c_in, p_in, m_in, k_in, l_in, density,
    c_out, p_out, m_out,
    c0, p0, m0, q0, lab, c1, p1, m1, q1, rate, fwd, bwd, part, gathered,
    load_sem, store_sem, send_sem, recv_sem, part_send, part_recv,
):
    group = lax.axis_index("groups")
    me = lax.axis_index("gx")
    left, right = lax.rem(me + n - 1, n), lax.rem(me + 1, n)
    tiles = layers // 8
    last = rows + 1
    first = (c0, p0, m0)
    second = (c1, p1, m1)
    ins = (c_in, p_in, m_in, l_in)
    outs = (c_out, p_out, m_out)

    loads = [
        pltpu.make_async_copy(src, dst.at[pl.ds(1, rows), pl.ds(PAD, layers), :], load_sem.at[i])
        for i, (src, dst) in enumerate(((c_in, c0), (p_in, p0), (l_in, lab), (m_in, m0)))
    ]
    loads.append(pltpu.make_async_copy(k_in, rate, load_sem.at[4]))
    for copy in loads:
        copy.start()

    barrier = pltpu.get_barrier_semaphore()

    @pl.loop(1, n)
    def _(d):
        pl.semaphore_signal(
            barrier, inc=1, device_id=(group, lax.rem(me + d, n)), device_id_type=MESH
        )

    def halo(step, way, f, j):
        z = pl.ds(PAD + 8 * j, 8)
        if step == 0:
            src = ins[f].at[0 if way == 0 else rows - 1, pl.ds(8 * j, 8), :]
            dst = (c0, p0, m0, lab)[f]
        else:
            src = second[f].at[1 if way == 0 else rows, z, :]
            dst = second[f]
        return pltpu.make_async_remote_copy(
            src_ref=src,
            dst_ref=dst.at[last if way == 0 else 0, z, :],
            send_sem=send_sem.at[step, way, f, j],
            recv_sem=recv_sem.at[step, way, f, j],
            device_id=(group, left if way == 0 else right),
            device_id_type=MESH,
        )

    has_left = me > 0
    has_right = me < n - 1

    for ref in (c0, p0, m0, q0, lab, c1, p1, m1, q1):
        zero = jnp.zeros((rows + 2, 8, width), ref.dtype)
        ref[:, 0:PAD, :] = zero
        ref[:, PAD + layers :, :] = zero

    @pl.when(jnp.logical_not(has_left))
    def _():
        for ref in (c0, p0, m0, lab, c1, p1, m1):
            ref[0, PAD : PAD + layers, :] = jnp.zeros((layers, width), ref.dtype)

    @pl.when(jnp.logical_not(has_right))
    def _():
        for ref in (c0, p0, m0, lab, c1, p1, m1):
            ref[last, PAD : PAD + layers, :] = jnp.zeros((layers, width), ref.dtype)

    pl.semaphore_wait(barrier, n - 1)

    def send_rows(j):
        for f in range(4):
            @pl.when(has_left)
            def _():
                halo(0, 0, f, j).start()

            @pl.when(has_right)
            def _():
                halo(0, 1, f, j).start()

    for j in range(AHEAD):
        send_rows(j)

    for copy in loads:
        copy.wait()

    def fold(v):
        total = v[:, 0:128]
        for at in range(128, width, 128):
            total = total + v[:, at : at + 128]
        return total

    def soak(labels, m):
        return jnp.where(labels >= 1, 1.0 / (1.0 + m * m), 0.0)

    def exchange(labels, c, p, x, z, shift):
        power = (shift - p) * LOG
        is_wall = labels == 2
        k = jnp.where(is_wall, rate[x - 1, pl.ds(z - PAD, 8), :], 0.0)
        forward = k * c * jnp.exp2(power)
        backward = k * jnp.exp2(-power)
        fwd[x - 1, pl.ds(z - PAD, 8), :] = forward
        bwd[x - 1, pl.ds(z - PAD, 8), :] = backward
        return fold(forward), fold(backward), fold(jnp.where(is_wall, 1.0, 0.0))

    def sum_start(step, sums):
        lane = lax.broadcasted_iota(jnp.int32, (1, 128), 1)
        a, b, w = (jnp.sum(jnp.sum(s, axis=0, keepdims=True), axis=1, keepdims=True) for s in sums)
        part[step] = jnp.where(lane == 0, a, jnp.where(lane == 1, b, jnp.where(lane == 2, w, 0.0)))

        @pl.loop(1, n)
        def _(d):
            pltpu.make_async_remote_copy(
                src_ref=part.at[step],
                dst_ref=gathered.at[step, d - 1],
                send_sem=part_send.at[step],
                recv_sem=part_recv.at[step],
                device_id=(group, lax.rem(me + d, n)),
                device_id_type=MESH,
            ).start()

    def sum_finish(step):
        all_parts = gathered.at[step]
        pltpu.make_async_copy(all_parts, all_parts, part_recv.at[step]).wait()
        total = part[step] + jnp.sum(gathered[step], axis=0)
        a, b, w = (total[:, i : i + 1] for i in range(3))
        delta = (density[0] * w + b - a) / (1.5 * (a + b))
        return delta, jnp.exp2(delta * LOG), jnp.exp2(-delta * LOG)

    def spread(src, q, x, i):
        z = PAD + 8 * i
        c_ref, p_ref, m_ref = src
        here = pl.ds(z, 8)
        c, p, m, labels, weight = (r[x, here, :] for r in (c_ref, p_ref, m_ref, lab, q))
        lane = lax.broadcasted_iota(jnp.int32, (8, width), 1)
        near = []
        for at in ((x - 1, here), (x + 1, here), (x, pl.ds(z - 1, 8)), (x, pl.ds(z + 1, 8))):
            near.append(tuple(r[at[0], at[1], :] for r in (c_ref, p_ref, m_ref, lab, q)))
        for shift, edge in ((1, 0), (width - 1, width - 1)):
            cb, pb, mb, lb, qb = (pltpu.roll(v, shift, 1) for v in (c, p, m, labels, weight))
            near.append((cb, pb, mb, jnp.where(lane == edge, 0, lb), jnp.where(lane == edge, 0.0, qb)))
        dc = dp = dm = None
        for cb, pb, mb, lb, qb in near:
            tc = qb * (cb - c)
            tp = jnp.where(lb == 2, pb - p, 0.0)
            tm = jnp.where(lb >= 1, mb - m, 0.0)
            dc, dp, dm = (tc, tp, tm) if dc is None else (dc + tc, dp + tp, dm + tm)
        is_open, is_wall = labels >= 1, labels == 2
        dc = weight * dc
        if i == 0:
            top = lax.broadcasted_iota(jnp.int32, (8, width), 0) == 0
            dm = jnp.where(top, dm - m, dm)
            dc = dc + jnp.where(jnp.logical_and(top, is_open), 1.0 - c, 0.0)
        if i == tiles - 1:
            bottom = lax.broadcasted_iota(jnp.int32, (8, width), 0) == 7
            dp = jnp.where(bottom, dp - p, dp)
        c = c + 0.16 * dc
        p = p + jnp.where(is_wall, 0.15 * dp, 0.0)
        m = m + jnp.where(is_open, 0.12 * dm, 0.0)
        return c, p, m

    def react(values, x, i, up, down):
        c, p, m = values
        z = pl.ds(8 * i, 8)
        reaction = fwd[x - 1, z, :] * up - bwd[x - 1, z, :] * down
        return c - 0.04 * reaction, p - 0.3 * reaction, m + 0.06 * reaction

    def put(dst, x, i, values):
        for ref, value in zip(dst, values):
            ref[x, pl.ds(PAD + 8 * i, 8), :] = value

    def get(src, x, i):
        return tuple(ref[x, pl.ds(PAD + 8 * i, 8), :] for ref in src)

    def add(sums, more):
        return tuple(s + t for s, t in zip(sums, more))

    none = (jnp.zeros((8, 128), jnp.float32),) * 3

    def opening(x, sums):
        for i in range(tiles):
            z = PAD + 8 * i
            c, p, m = get(first, x, i)
            labels = lab[x, pl.ds(z, 8), :]
            q0[x, pl.ds(z, 8), :] = soak(labels, m)
            sums = add(sums, exchange(labels, c, p, x, z, 0.0))
        return sums

    sum_start(0, lax.fori_loop(1, rows + 1, opening, none))
    for j in range(AHEAD, tiles):
        send_rows(j)

    @pl.loop(2, rows)
    def _(x):
        for i in range(tiles):
            put(second, x, i, spread(first, q0, x, i))

    shift, up, down = sum_finish(0)
    shift_s, up_s, down_s = shift[0, 0], up[0, 0], down[0, 0]

    def settle(values, x, i):
        z = PAD + 8 * i
        c, p, m = react(values, x, i, up_s, down_s)
        put(second, x, i, (c, p, m))
        labels = lab[x, pl.ds(z, 8), :]
        q1[x, pl.ds(z, 8), :] = soak(labels, m)
        return exchange(labels, c, p, x, z, shift_s)

    def inner(i, sums):
        return lax.fori_loop(2, rows, lambda x, s: add(s, settle(get(second, x, i), x, i)), sums)

    sums = none
    sides = ((0, 1, 1, has_left), (last, rows, 0, has_right))
    for i in range(tiles):
        if i == tiles - 1:
            sums = inner(i, sums)
        for outer, x, way, present in sides:
            @pl.when(present)
            def _():
                for f in range(4):
                    halo(0, way, f, i).wait_recv()

            z = pl.ds(PAD + 8 * i, 8)
            q0[outer, z, :] = soak(lab[outer, z, :], m0[outer, z, :])
            sums = add(sums, settle(spread(first, q0, x, i), x, i))

            @pl.when(present)
            def _():
                for f in range(3):
                    halo(1, 1 - way, f, i).start()

        if i < tiles - 1:
            sums = inner(i, sums)

    sum_start(1, sums)

    @pl.loop(2, rows)
    def _(x):
        for i in range(tiles):
            put(first, x, i, spread(second, q1, x, i))

    _, up, down = sum_finish(1)
    up_f, down_f = up[0, 0], down[0, 0]

    @pl.loop(2, rows)
    def _(x):
        for i in range(tiles):
            put(first, x, i, react(get(first, x, i), x, i, up_f, down_f))

    stores = []
    for f in range(3):
        stores.append(
            pltpu.make_async_copy(
                first[f].at[pl.ds(2, rows - 2), pl.ds(PAD, layers), :],
                outs[f].at[pl.ds(1, rows - 2), :, :],
                store_sem.at[f, 0],
            )
        )
        stores[-1].start()

    for i in range(tiles):
        for outer, x, way, present in sides:
            @pl.when(present)
            def _():
                for f in range(3):
                    halo(1, way, f, i).wait_recv()

            z = pl.ds(PAD + 8 * i, 8)
            q1[outer, z, :] = soak(lab[outer, z, :], m1[outer, z, :])
            put(first, x, i, react(spread(second, q1, x, i), x, i, up_f, down_f))
            for f in range(3):
                stores.append(
                    pltpu.make_async_copy(
                        first[f].at[x, z, :],
                        outs[f].at[x - 1, pl.ds(8 * i, 8), :],
                        store_sem.at[f, 1 + 2 * i + way],
                    )
                )
                stores[-1].start()

    for step in range(2):
        pltpu.make_async_copy(gathered.at[step], gathered.at[step], part_send.at[step]).wait()
        for outer, x, way, present in sides:
            @pl.when(present)
            def _():
                for i in range(tiles):
                    for f in range(4 - step):
                        halo(step, 1 - way, f, i).wait_send()
    for copy in stores:
        copy.wait()


def hand_out(*refs):
    sources, targets, held, sem = refs[:3], refs[3:6], refs[6:9], refs[9]
    q = sources[0].shape[0] // 4
    todo = []
    for h in range(4):
        for f in range(3):
            piece = pl.ds(h * q, q)
            a = pltpu.make_async_copy(sources[f].at[piece], held[f].at[piece], sem.at[0, f, h])
            b = pltpu.make_async_copy(held[f].at[piece], targets[f].at[piece], sem.at[1, f, h])
            a.start()
            todo.append((a, b))
    for a, b in todo:
        a.wait()
        b.start()
    for a, b in todo:
        b.wait()


def solution(mesh):
    n = mesh.shape["gx"]

    def on_device(oxygen, potential, moisture, rate_constant, cell_labels, current_density):
        rows, layers, width = oxygen.shape
        tiles = layers // 8
        padded = (rows + 2, layers + 2 * PAD, width)
        big = pltpu.VMEM(padded, jnp.float32)
        own = pltpu.VMEM((rows, layers, width), jnp.float32)
        hbm = pl.BlockSpec(memory_space=pl.ANY)
        pinned = pl.BlockSpec(memory_space=pltpu.HBM)
        fields = pl.pallas_call(
            functools.partial(kernel, n, rows, layers, width),
            out_shape=[jax.ShapeDtypeStruct((rows, layers, width), jnp.float32)] * 3,
            in_specs=[pinned] * 5 + [pl.BlockSpec(memory_space=pltpu.SMEM)],
            out_specs=[hbm] * 3,
            scratch_shapes=[
                big, big, big, big, pltpu.VMEM(padded, jnp.int32),
                big, big, big, big,
                own, own, own,
                pltpu.VMEM((2, 1, 128), jnp.float32),
                pltpu.VMEM((2, n - 1, 1, 128), jnp.float32),
                pltpu.SemaphoreType.DMA((5,)),
                pltpu.SemaphoreType.DMA((3, 1 + 2 * tiles)),
                pltpu.SemaphoreType.DMA((2, 2, 4, tiles)),
                pltpu.SemaphoreType.DMA((2, 2, 4, tiles)),
                pltpu.SemaphoreType.DMA((2,)),
                pltpu.SemaphoreType.DMA((2,)),
            ],
            compiler_params=pltpu.CompilerParams(
                collective_id=0, has_side_effects=True, vmem_limit_bytes=63 * 1024 * 1024 + 512 * 1024
            ),
        )(oxygen, potential, moisture, rate_constant, cell_labels, current_density)
        return pl.pallas_call(
            hand_out,
            out_shape=[jax.ShapeDtypeStruct((rows, layers, width), jnp.float32)] * 3,
            in_specs=[hbm] * 3,
            out_specs=[pinned] * 3,
            scratch_shapes=[own, own, own, pltpu.SemaphoreType.DMA((2, 3, 4))],
            compiler_params=pltpu.CompilerParams(vmem_limit_bytes=62 * 1024 * 1024),
        )(*fields)

    field = P(("groups", "gx"), None, None)
    return jax.shard_map(
        on_device,
        mesh=mesh,
        in_specs=(field,) * 5 + (P("groups"),),
        out_specs=(field,) * 3,
        check_vma=False,
    )
```
